32 devices in a mesh: grp: 2 (over y), fib: 4 (over z), slab: 2 (over x), var: 2 (over core).
Axes of the slice: x: 2, y: 2, z: 4, core: 2. Of those that a mesh axis runs over, the one named last changes fastest.
Arguments:
- field: bfloat16 [32, 512, 64, 256], P(('grp', 'var'), 'fib', 'slab'), parts along dimension 0, may hold values from -800 to 800
- rank: int32 [32], P(('grp', 'var')), parts along dimension 0, may hold values from 32 to 128
- start_basis: float32 [512, 128], replicated, may hold values from -6 to 6
Outputs:
- rebuilt: bfloat16 [32, 512, 64, 256], P(('grp', 'var'), 'fib', 'slab'), parts along dimension 0
The draws below stay inside these ranges and needn't reach their ends.
There are 2 independent parts, one for each index of `grp`. The reference program is written for one: setup_inputs(seed, part) draws one part's arguments, and reference() takes and returns one part's arrays. A program takes and returns all parts, laid end to end along the dimension named above; an argument that names none is the same for every part. Nothing has to cross between parts.
All inputs are finite; a program needn't handle non-finite values.
Results may differ from the reference program's by a relative error of at most 0.0062.
Values may be sent and summed in bfloat16 or wider, within the bound.
A program may use at most 192 MiB of HBM per device.

```python
import math
import jax
import jax.numpy as jnp
from jax import lax

V = 16
I1 = 512
RMAX = 128
I2 = 256
ITERS = 4
I3 = 64


def draw_field(key, part):
    key = jax.random.fold_in(key, 11)
    keys = jax.random.split(key, 7)
    row_scale = jnp.exp(jax.random.uniform(keys[0], (1, I1, 1, 1), jnp.float32) * math.log(10.0))
    var_scale = jnp.exp(jax.random.uniform(keys[1], (V, 1, 1, 1), jnp.float32) * math.log(3.0))
    depth = 1.0 + 2.0 * jnp.arange(I3, dtype=jnp.float32).reshape(1, 1, I3, 1) / I3
    load_a = jnp.clip(jax.random.normal(keys[2], (1, I1, 1, 1), jnp.float32), -4.0, 4.0)
    load_b = jnp.clip(jax.random.normal(keys[3], (1, I1, 1, 1), jnp.float32), -4.0, 4.0)
    shared_a = jnp.clip(jax.random.normal(keys[4], (V, 1, I3, I2), jnp.float32), -4.0, 4.0)
    shared_b = jnp.clip(jax.random.normal(keys[5], (V, 1, I3, I2), jnp.float32), -4.0, 4.0)
    noise = jnp.clip(jax.random.normal(keys[6], (V, I1, I3, I2), jnp.float32), -6.0, 6.0)
    mix = 0.7
    value = 0.15 * row_scale * var_scale * depth * (noise + mix * (load_a * shared_a + load_b * shared_b))
    return value.astype(jnp.bfloat16)


def with_ends(values, rng, low, largest):
    index_at = [jax.random.randint(jax.random.fold_in(rng, axis), (), 0, length) for axis, length in enumerate(values.shape)]
    longest = values.shape.index(max(values.shape))
    neighbour = index_at[:longest] + [(index_at[longest] + 1) % values.shape[longest]] + index_at[longest + 1:]
    return values.at[tuple(index_at)].set(low).at[tuple(neighbour)].set(largest)


def scatter_about(key, extent, deviation, bound, kind=jnp.bfloat16):
    return jnp.clip(deviation * jax.random.normal(key, extent, jnp.float32), -bound, bound).astype(kind)


def setup_inputs(seed: int = 0, part: int = 0) -> dict:
    seeds = jax.random.split(jax.random.key(seed), 4)
    part_keys = jax.random.split(jax.random.fold_in(seeds[3], part), 4)
    field = draw_field(jax.random.fold_in(jax.random.fold_in(seeds[3], part), 71), part)
    rank = with_ends(jax.random.randint(part_keys[1], (V,), RMAX // 4, RMAX + 1), jax.random.fold_in(part_keys[1], 1), RMAX // 4, RMAX).astype(jnp.int32)
    start_basis = scatter_about(seeds[2], (I1, RMAX), 1.0, 6.0, jnp.float32)
    return dict(field=field, rank=rank, start_basis=start_basis)


def orthonormal(block):
    small = jnp.dot(block.T, block, precision=lax.Precision.HIGHEST)
    factor = jnp.linalg.cholesky(small)
    return lax.linalg.triangular_solve(factor, block, left_side=False, lower=True, transpose_a=True)

def reference(field, rank, start_basis):

    def partial_gram(plane):
        matrix = plane.reshape(I1, I3 * I2)
        return jnp.dot(matrix.astype(jnp.float32), matrix.T.astype(jnp.float32), preferred_element_type=jnp.float32)
    gram = jnp.sum(lax.map(partial_gram, field), axis=0)
    basis = orthonormal(start_basis)
    for step in range(ITERS):
        basis = orthonormal(jnp.dot(gram, basis, precision=lax.Precision.HIGHEST))

    def rebuild(pair):
        plane, limit = pair
        keep = (jnp.arange(RMAX, dtype=jnp.int32) < limit).astype(basis.dtype)
        basis_bf = (basis * keep[None, :]).astype(jnp.bfloat16)
        matrix = plane.reshape(I1, I3 * I2)
        core = jnp.dot(basis_bf.T.astype(jnp.float32), matrix.astype(jnp.float32), preferred_element_type=jnp.float32).astype(jnp.bfloat16)
        result = jnp.dot(basis_bf.astype(jnp.float32), core.astype(jnp.float32), preferred_element_type=jnp.float32).astype(jnp.bfloat16)
        return result.reshape(I1, I3, I2)
    return lax.map(rebuild, (field, rank))
```

```python
import functools

import jax
import jax.numpy as jnp
from jax import lax
from jax.experimental import pallas as pl
from jax.experimental.pallas import tpu as pltpu
from jax.sharding import PartitionSpec as P

ITERS = 4
MESH = pl.DeviceIdType.MESH
ANY = pl.BlockSpec(memory_space=pl.ANY)
VMEM = pl.BlockSpec(memory_space=pltpu.VMEM)
WINDOW = 3


def greet(axis, peers):
    barrier = pltpu.get_barrier_semaphore()
    for peer in peers:
        pl.semaphore_signal(barrier, inc=1, device_id={axis: peer}, device_id_type=MESH)
    pl.semaphore_wait(barrier, len(peers))


def exchange_kernel(n, flat, fibres, gram, held, send_sem, recv_sem, own_sem, load_sem):
    nvars, rows, _ = flat.shape
    share = fibres.shape[2]
    tile = min(share, 512)
    me = lax.axis_index("fib")
    greet("fib", [lax.rem(me + off, n) for off in range(1, n)])
    gram[...] = jnp.zeros_like(gram)

    def place(who, length):
        return pl.ds(pl.multiple_of(who * length, length), length)

    def remote(v, off):
        peer = lax.rem(me + off, n)
        return pltpu.make_async_remote_copy(
            src_ref=flat.at[v, :, place(peer, share)],
            dst_ref=fibres.at[v, place(me, rows), :],
            send_sem=send_sem.at[v, off],
            recv_sem=recv_sem.at[v, off],
            device_id={"fib": peer},
            device_id_type=MESH,
        )

    def arrival(v, off):
        source = lax.rem(me + n - off, n)
        return pltpu.make_async_remote_copy(
            src_ref=flat.at[v, :, place(me, share)],
            dst_ref=fibres.at[v, place(source, rows), :],
            send_sem=send_sem.at[v, off],
            recv_sem=recv_sem.at[v, off],
            device_id={"fib": lax.rem(me + off, n)},
            device_id_type=MESH,
        )

    def own(v):
        return pltpu.make_async_copy(
            flat.at[v, :, place(me, share)], fibres.at[v, place(me, rows), :], own_sem.at[v]
        )

    def start(v):
        own(v).start()
        pl.loop(1, n)(lambda off: remote(v, off).start())

    def finish(v):
        own(v).wait()

        @pl.loop(1, n)
        def _(off):
            remote(v, off).wait_send()
            arrival(v, off).wait_recv()

        load = pltpu.make_async_copy(fibres.at[v], held, load_sem)
        load.start()
        load.wait()

        @pl.loop(0, share // tile)
        def _(t):
            block = held[:, pl.ds(pl.multiple_of(t * tile, tile), tile)]
            gram[...] += lax.dot_general(
                block, block, (((1,), (1,)), ((), ())), preferred_element_type=jnp.float32
            )

    @pl.loop(0, nvars + WINDOW)
    def _(step):
        pl.when(step < nvars)(lambda: start(step))
        pl.when(step >= WINDOW)(lambda: finish(step - WINDOW))


def exchange(flat, n):
    nvars, rows, columns = flat.shape
    whole, share = rows * n, columns // n
    return pl.pallas_call(
        functools.partial(exchange_kernel, n),
        out_shape=(
            jax.ShapeDtypeStruct((nvars, whole, share), flat.dtype),
            jax.ShapeDtypeStruct((whole, whole), jnp.float32),
        ),
        in_specs=[ANY],
        out_specs=(ANY, VMEM),
        scratch_shapes=[
            pltpu.VMEM((whole, share), flat.dtype),
            pltpu.SemaphoreType.DMA((nvars, n)),
            pltpu.SemaphoreType.DMA((nvars, n)),
            pltpu.SemaphoreType.DMA((nvars,)),
            pltpu.SemaphoreType.DMA,
        ],
        compiler_params=pltpu.CompilerParams(
            collective_id=0, has_side_effects=True, vmem_limit_bytes=32 * 2**20
        ),
        name="exchange",
    )(flat)


def reduce_kernel(axes, part, total, held, *scratch):
    lands, sems = scratch[: len(axes)], scratch[len(axes):]
    barrier = pltpu.get_barrier_semaphore()
    count = 0
    for axis, n in axes:
        me = lax.axis_index(axis)
        for off in range(1, n):
            pl.semaphore_signal(
                barrier, inc=1, device_id={axis: lax.rem(me + off, n)}, device_id_type=MESH
            )
            count += 1
    pl.semaphore_wait(barrier, count)
    base, length = 0, total.shape[0]
    levels = []
    for level, (axis, n) in enumerate(axes):
        me = lax.axis_index(axis)
        size = length // n
        levels.append((axis, n, me, base, size))
        source = held if level else part
        copies = []
        for off in range(1, n):
            peer = lax.rem(me + off, n)
            copies.append(
                pltpu.make_async_remote_copy(
                    src_ref=source.at[pl.ds(pl.multiple_of(base + peer * size, size), size), :],
                    dst_ref=lands[level].at[off - 1],
                    send_sem=sems[0].at[level, off],
                    recv_sem=sems[1].at[level, off],
                    device_id={axis: peer},
                    device_id_type=MESH,
                )
            )
            copies[-1].start()
        base = base + me * size
        length = size
        for copy in copies:
            copy.wait()
        mine = pl.ds(pl.multiple_of(base, size), size)
        value = source[mine, :]
        for off in range(1, n):
            value += lands[level][off - 1]
        target = held if level < len(axes) - 1 else total
        target[mine, :] = value
    for level in reversed(range(len(axes))):
        axis, n, me, start, size = levels[level]
        mine = pl.ds(pl.multiple_of(start + me * size, size), size)
        sends = []
        for off in range(1, n):
            peer = lax.rem(me + off, n)
            sends.append(
                pltpu.make_async_remote_copy(
                    src_ref=total.at[mine, :],
                    dst_ref=total.at[mine, :],
                    send_sem=sems[2].at[level, off],
                    recv_sem=sems[3].at[level, off],
                    device_id={axis: peer},
                    device_id_type=MESH,
                )
            )
            sends[-1].start()
        for off in range(1, n):
            source = lax.rem(me + n - off, n)
            theirs = pl.ds(pl.multiple_of(start + source * size, size), size)
            sends[off - 1].wait_send()
            pltpu.make_async_remote_copy(
                src_ref=total.at[mine, :],
                dst_ref=total.at[theirs, :],
                send_sem=sems[2].at[level, off],
                recv_sem=sems[3].at[level, off],
                device_id={axis: lax.rem(me + off, n)},
                device_id_type=MESH,
            ).wait_recv()


def reduce_all(part, axes):
    rows, columns = part.shape
    total = 1
    for _, n in axes:
        total *= n
    if rows % (8 * total):
        return lax.psum(part, tuple(axis for axis, _ in axes))
    lands, size = [], rows
    for _, n in axes:
        size //= n
        lands.append(pltpu.VMEM((n - 1, size, columns), jnp.float32))
    sem = pltpu.SemaphoreType.DMA((len(axes), max(n for _, n in axes)))
    return pl.pallas_call(
        functools.partial(reduce_kernel, axes),
        out_shape=jax.ShapeDtypeStruct(part.shape, part.dtype),
        in_specs=[VMEM],
        out_specs=VMEM,
        scratch_shapes=[pltpu.VMEM(part.shape, jnp.float32)] + lands + [sem] * 4,
        compiler_params=pltpu.CompilerParams(
            collective_id=1, has_side_effects=True, vmem_limit_bytes=32 * 2**20
        ),
        name="reduce_all",
    )(part)


def rebuild_kernel(n, core, left_factor, out, full, stage, send_sem, recv_sem, own_sem, out_sem):
    nvars, depth, share = core.shape
    rows = left_factor.shape[1]
    me = lax.axis_index("fib")
    barrier = pltpu.get_barrier_semaphore()
    has_left, has_right = me > 0, me < n - 1
    lo, hi = me - 1, me + 1

    for flag, peer in ((has_left, lo), (has_right, hi)):

        @pl.when(flag)
        def _():
            pl.semaphore_signal(barrier, inc=1, device_id={"fib": peer}, device_id_type=MESH)

    inner = has_left & has_right
    pl.when(inner)(lambda: pl.semaphore_wait(barrier, 2))
    pl.when(jnp.logical_not(inner))(lambda: pl.semaphore_wait(barrier, 1))

    def columns(who):
        return pl.ds(pl.multiple_of(who * share, share), share)

    def copy(v, who, side, peer):
        piece = full.at[v, :, columns(who)]
        return pltpu.make_async_remote_copy(
            src_ref=piece,
            dst_ref=piece,
            send_sem=send_sem.at[side, v, who],
            recv_sem=recv_sem.at[v, who],
            device_id={"fib": peer},
            device_id_type=MESH,
        )

    def fetch(v):
        return pltpu.make_async_copy(core.at[v], full.at[v, :, columns(me)], own_sem.at[v])

    def to_right(v, who):
        return copy(v, who, 1, hi)

    def to_left(v, who):
        return copy(v, who, 0, lo)

    def write(slot, v, who):
        return pltpu.make_async_copy(
            stage.at[slot], out.at[v, :, columns(who)], out_sem.at[slot]
        )

    def rebuild(slot, v, who, first):
        pl.when(jnp.logical_not(first))(lambda: write(slot, v, who).wait())
        tile = min(share, 512)

        @pl.loop(0, share // tile)
        def _(t):
            at = pl.ds(pl.multiple_of(t * tile, tile), tile)
            source = pl.ds(pl.multiple_of(who * share + t * tile, tile), tile)
            stage[slot, :, at] = jnp.dot(
                left_factor[v], full[v, :, source], preferred_element_type=jnp.float32
            ).astype(stage.dtype)

        write(slot, v, who).start()

    pl.loop(0, nvars)(lambda v: fetch(v).start())

    @pl.loop(0, nvars)
    def _(v):
        fetch(v).wait()
        pl.when(has_left)(lambda: to_left(v, me).start())
        pl.when(has_right)(lambda: to_right(v, me).start())

    pl.loop(0, nvars)(lambda v: rebuild(2, v, me, v == 0))
    write(2, 0, me).wait()

    for hop in range(1, n):
        from_left, from_right = me - hop, me + hop
        left_ok, right_ok = from_left >= 0, from_right < n

        @pl.loop(0, nvars)
        def _(v):
            @pl.when(left_ok)
            def _():
                to_right(v, from_left).wait_recv()
                pl.when(has_right)(lambda: to_right(v, from_left).start())

            @pl.when(right_ok)
            def _():
                to_left(v, from_right).wait_recv()
                pl.when(has_left)(lambda: to_left(v, from_right).start())

            pl.when(left_ok)(lambda: rebuild(0, v, from_left, v == 0))
            pl.when(right_ok)(lambda: rebuild(1, v, from_right, v == 0))

        pl.when(left_ok)(lambda: write(0, 0, from_left).wait())
        pl.when(right_ok)(lambda: write(1, 0, from_right).wait())

    for hop in range(n):
        from_left, from_right = me - hop, me + hop

        @pl.loop(0, nvars)
        def _(v):
            pl.when((from_left >= 0) & has_right)(lambda: to_right(v, from_left).wait_send())
            pl.when((from_right < n) & has_left)(lambda: to_left(v, from_right).wait_send())


def rebuild_all(core, left_factor, n):
    nvars, depth, share = core.shape
    rows = left_factor.shape[1]
    return pl.pallas_call(
        functools.partial(rebuild_kernel, n),
        out_shape=jax.ShapeDtypeStruct((nvars, rows, share * n), core.dtype),
        in_specs=[ANY, VMEM],
        out_specs=ANY,
        scratch_shapes=[
            pltpu.VMEM((nvars, depth, share * n), core.dtype),
            pltpu.VMEM((3, rows, share), core.dtype),
            pltpu.SemaphoreType.DMA((2, nvars, n)),
            pltpu.SemaphoreType.DMA((nvars, n)),
            pltpu.SemaphoreType.DMA((nvars,)),
            pltpu.SemaphoreType.DMA((3,)),
        ],
        compiler_params=pltpu.CompilerParams(
            collective_id=2, has_side_effects=True, vmem_limit_bytes=48 * 2**20
        ),
        name="rebuild_all",
    )(core, left_factor)


def orthonormal(block):
    small = jnp.dot(block.T, block, precision=lax.Precision.HIGHEST)
    factor = jnp.linalg.cholesky(small)
    return lax.linalg.triangular_solve(factor, block, left_side=False, lower=True, transpose_a=True)


def on_device(sizes, field, rank, start_basis):
    nvars, rows, depth, width = field.shape
    n = sizes["fib"]
    flat = field.reshape(nvars, rows, depth * width)
    fibres, partial_gram = exchange(flat, n)
    gram = reduce_all(partial_gram, tuple((axis, sizes[axis]) for axis in ("var", "slab", "fib")))
    basis = orthonormal(start_basis)
    for step in range(ITERS):
        basis = orthonormal(jnp.dot(gram, basis, precision=lax.Precision.HIGHEST))
    columns = jnp.arange(basis.shape[1], dtype=jnp.int32)
    keep = (columns[None, :] < rank[:, None]).astype(basis.dtype)
    basis_bf = (basis[None, :, :] * keep[:, None, :]).astype(jnp.bfloat16)
    core = jnp.einsum("vir,vic->vrc", basis_bf, fibres, preferred_element_type=jnp.float32).astype(
        jnp.bfloat16
    )
    own_rows = lax.dynamic_slice_in_dim(basis_bf, lax.axis_index("fib") * rows, rows, 1)
    result = rebuild_all(core, own_rows, n)
    return result.reshape(nvars, rows, depth, width)


def solution(mesh):
    return jax.shard_map(
        functools.partial(on_device, dict(mesh.shape)),
        mesh=mesh,
        in_specs=(P(("grp", "var"), "fib", "slab", None), P(("grp", "var")), P()),
        out_specs=P(("grp", "var"), "fib", "slab", None),
        check_vma=False,
    )
```

```python
import functools

import jax
import jax.numpy as jnp
from jax import lax
from jax.experimental import pallas as pl
from jax.experimental.pallas import tpu as pltpu
from jax.sharding import PartitionSpec as P

ITERS = 4
MESH = pl.DeviceIdType.MESH
ANY = pl.BlockSpec(memory_space=pl.ANY)
VMEM = pl.BlockSpec(memory_space=pltpu.VMEM)
WINDOW = 3


def greet(axis, peers):
    barrier = pltpu.get_barrier_semaphore()
    for peer in peers:
        pl.semaphore_signal(barrier, inc=1, device_id={axis: peer}, device_id_type=MESH)
    pl.semaphore_wait(barrier, len(peers))


def exchange_kernel(n, flat, fibres, gram, held, send_sem, recv_sem, own_sem, load_sem):
    nvars, rows, _ = flat.shape
    share = fibres.shape[2]
    tile = min(share, 512)
    me = lax.axis_index("fib")
    greet("fib", [lax.rem(me + off, n) for off in range(1, n)])
    gram[...] = jnp.zeros_like(gram)

    def place(who, length):
        return pl.ds(pl.multiple_of(who * length, length), length)

    def remote(v, off):
        peer = lax.rem(me + off, n)
        return pltpu.make_async_remote_copy(
            src_ref=flat.at[v, :, place(peer, share)],
            dst_ref=fibres.at[v, place(me, rows), :],
            send_sem=send_sem.at[v, off],
            recv_sem=recv_sem.at[v, off],
            device_id={"fib": peer},
            device_id_type=MESH,
        )

    def arrival(v, off):
        source = lax.rem(me + n - off, n)
        return pltpu.make_async_remote_copy(
            src_ref=flat.at[v, :, place(me, share)],
            dst_ref=fibres.at[v, place(source, rows), :],
            send_sem=send_sem.at[v, off],
            recv_sem=recv_sem.at[v, off],
            device_id={"fib": lax.rem(me + off, n)},
            device_id_type=MESH,
        )

    def own(v):
        return pltpu.make_async_copy(
            flat.at[v, :, place(me, share)], fibres.at[v, place(me, rows), :], own_sem.at[v]
        )

    def start(v):
        own(v).start()
        pl.loop(1, n)(lambda off: remote(v, off).start())

    def finish(v):
        own(v).wait()

        @pl.loop(1, n)
        def _(off):
            remote(v, off).wait_send()
            arrival(v, off).wait_recv()

        load = pltpu.make_async_copy(fibres.at[v], held, load_sem)
        load.start()
        load.wait()

        @pl.loop(0, share // tile)
        def _(t):
            block = held[:, pl.ds(pl.multiple_of(t * tile, tile), tile)]
            gram[...] += lax.dot_general(
                block, block, (((1,), (1,)), ((), ())), preferred_element_type=jnp.float32
            )

    @pl.loop(0, nvars + WINDOW)
    def _(step):
        pl.when(step < nvars)(lambda: start(step))
        pl.when(step >= WINDOW)(lambda: finish(step - WINDOW))


def exchange(flat, n):
    nvars, rows, columns = flat.shape
    whole, share = rows * n, columns // n
    return pl.pallas_call(
        functools.partial(exchange_kernel, n),
        out_shape=(
            jax.ShapeDtypeStruct((nvars, whole, share), flat.dtype),
            jax.ShapeDtypeStruct((whole, whole), jnp.float32),
        ),
        in_specs=[ANY],
        out_specs=(ANY, VMEM),
        scratch_shapes=[
            pltpu.VMEM((whole, share), flat.dtype),
            pltpu.SemaphoreType.DMA((nvars, n)),
            pltpu.SemaphoreType.DMA((nvars, n)),
            pltpu.SemaphoreType.DMA((nvars,)),
            pltpu.SemaphoreType.DMA,
        ],
        compiler_params=pltpu.CompilerParams(
            collective_id=0, has_side_effects=True, vmem_limit_bytes=32 * 2**20
        ),
        name="exchange",
    )(flat)


def reduce_kernel(axes, part, total, held, *scratch):
    lands, sems = scratch[: len(axes)], scratch[len(axes):]
    barrier = pltpu.get_barrier_semaphore()
    count = 0
    for axis, n in axes:
        me = lax.axis_index(axis)
        for off in range(1, n):
            pl.semaphore_signal(
                barrier, inc=1, device_id={axis: lax.rem(me + off, n)}, device_id_type=MESH
            )
            count += 1
    pl.semaphore_wait(barrier, count)
    base, length = 0, total.shape[0]
    levels = []
    for level, (axis, n) in enumerate(axes):
        me = lax.axis_index(axis)
        size = length // n
        levels.append((axis, n, me, base, size))
        source = held if level else part
        copies = []
        for off in range(1, n):
            peer = lax.rem(me + off, n)
            copies.append(
                pltpu.make_async_remote_copy(
                    src_ref=source.at[pl.ds(pl.multiple_of(base + peer * size, size), size), :],
                    dst_ref=lands[level].at[off - 1],
                    send_sem=sems[0].at[level, off],
                    recv_sem=sems[1].at[level, off],
                    device_id={axis: peer},
                    device_id_type=MESH,
                )
            )
            copies[-1].start()
        base = base + me * size
        length = size
        for copy in copies:
            copy.wait()
        mine = pl.ds(pl.multiple_of(base, size), size)
        value = source[mine, :]
        for off in range(1, n):
            value += lands[level][off - 1]
        target = held if level < len(axes) - 1 else total
        target[mine, :] = value
    for level in reversed(range(len(axes))):
        axis, n, me, start, size = levels[level]
        mine = pl.ds(pl.multiple_of(start + me * size, size), size)
        sends = []
        for off in range(1, n):
            peer = lax.rem(me + off, n)
            sends.append(
                pltpu.make_async_remote_copy(
                    src_ref=total.at[mine, :],
                    dst_ref=total.at[mine, :],
                    send_sem=sems[2].at[level, off],
                    recv_sem=sems[3].at[level, off],
                    device_id={axis: peer},
                    device_id_type=MESH,
                )
            )
            sends[-1].start()
        for off in range(1, n):
            source = lax.rem(me + n - off, n)
            theirs = pl.ds(pl.multiple_of(start + source * size, size), size)
            sends[off - 1].wait_send()
            pltpu.make_async_remote_copy(
                src_ref=total.at[mine, :],
                dst_ref=total.at[theirs, :],
                send_sem=sems[2].at[level, off],
                recv_sem=sems[3].at[level, off],
                device_id={axis: lax.rem(me + off, n)},
                device_id_type=MESH,
            ).wait_recv()


def reduce_all(part, axes):
    rows, columns = part.shape
    total = 1
    for _, n in axes:
        total *= n
    if rows % (8 * total):
        return lax.psum(part, tuple(axis for axis, _ in axes))
    lands, size = [], rows
    for _, n in axes:
        size //= n
        lands.append(pltpu.VMEM((n - 1, size, columns), jnp.float32))
    sem = pltpu.SemaphoreType.DMA((len(axes), max(n for _, n in axes)))
    return pl.pallas_call(
        functools.partial(reduce_kernel, axes),
        out_shape=jax.ShapeDtypeStruct(part.shape, part.dtype),
        in_specs=[VMEM],
        out_specs=VMEM,
        scratch_shapes=[pltpu.VMEM(part.shape, jnp.float32)] + lands + [sem] * 4,
        compiler_params=pltpu.CompilerParams(
            collective_id=1, has_side_effects=True, vmem_limit_bytes=32 * 2**20
        ),
        name="reduce_all",
    )(part)


def rebuild_kernel(n, core, left_factor, out, full, stage, send_sem, recv_sem, own_sem, out_sem):
    nvars, depth, share = core.shape
    rows = left_factor.shape[1]
    me = lax.axis_index("fib")
    barrier = pltpu.get_barrier_semaphore()
    has_left, has_right = me > 0, me < n - 1
    lo, hi = me - 1, me + 1

    for flag, peer in ((has_left, lo), (has_right, hi)):

        @pl.when(flag)
        def _():
            pl.semaphore_signal(barrier, inc=1, device_id={"fib": peer}, device_id_type=MESH)

    inner = has_left & has_right
    pl.when(inner)(lambda: pl.semaphore_wait(barrier, 2))
    pl.when(jnp.logical_not(inner))(lambda: pl.semaphore_wait(barrier, 1))

    def columns(who):
        return pl.ds(pl.multiple_of(who * share, share), share)

    def copy(v, who, side, peer):
        piece = full.at[v, :, columns(who)]
        return pltpu.make_async_remote_copy(
            src_ref=piece,
            dst_ref=piece,
            send_sem=send_sem.at[side, v, who],
            recv_sem=recv_sem.at[v, who],
            device_id={"fib": peer},
            device_id_type=MESH,
        )

    def fetch(v):
        return pltpu.make_async_copy(core.at[v], full.at[v, :, columns(me)], own_sem.at[v])

    def to_right(v, who):
        return copy(v, who, 1, hi)

    def to_left(v, who):
        return copy(v, who, 0, lo)

    def write(slot, v, who):
        return pltpu.make_async_copy(
            stage.at[slot], out.at[v, :, columns(who)], out_sem.at[slot]
        )

    def rebuild(slot, v, who, first):
        pl.when(jnp.logical_not(first))(lambda: write(slot, v, who).wait())
        tile = min(share, 512)

        @pl.loop(0, share // tile)
        def _(t):
            at = pl.ds(pl.multiple_of(t * tile, tile), tile)
            source = pl.ds(pl.multiple_of(who * share + t * tile, tile), tile)
            stage[slot, :, at] = jnp.dot(
                left_factor[v], full[v, :, source], preferred_element_type=jnp.float32
            ).astype(stage.dtype)

        write(slot, v, who).start()

    pl.loop(0, nvars)(lambda v: fetch(v).start())

    @pl.loop(0, nvars)
    def _(v):
        fetch(v).wait()
        pl.when(has_left)(lambda: to_left(v, me).start())
        pl.when(has_right)(lambda: to_right(v, me).start())

    pl.loop(0, nvars)(lambda v: rebuild(2, v, me, v == 0))
    write(2, 0, me).wait()

    for hop in range(1, n):
        from_left, from_right = me - hop, me + hop
        left_ok, right_ok = from_left >= 0, from_right < n

        @pl.loop(0, nvars)
        def _(v):
            @pl.when(left_ok)
            def _():
                to_right(v, from_left).wait_recv()
                pl.when(has_right)(lambda: to_right(v, from_left).start())

            @pl.when(right_ok)
            def _():
                to_left(v, from_right).wait_recv()
                pl.when(has_left)(lambda: to_left(v, from_right).start())

            pl.when(left_ok)(lambda: rebuild(0, v, from_left, v == 0))
            pl.when(right_ok)(lambda: rebuild(1, v, from_right, v == 0))

        pl.when(left_ok)(lambda: write(0, 0, from_left).wait())
        pl.when(right_ok)(lambda: write(1, 0, from_right).wait())

    for hop in range(n):
        from_left, from_right = me - hop, me + hop

        @pl.loop(0, nvars)
        def _(v):
            pl.when((from_left >= 0) & has_right)(lambda: to_right(v, from_left).wait_send())
            pl.when((from_right < n) & has_left)(lambda: to_left(v, from_right).wait_send())


def rebuild_all(core, left_factor, n):
    nvars, depth, share = core.shape
    rows = left_factor.shape[1]
    return pl.pallas_call(
        functools.partial(rebuild_kernel, n),
        out_shape=jax.ShapeDtypeStruct((nvars, rows, share * n), core.dtype),
        in_specs=[ANY, VMEM],
        out_specs=ANY,
        scratch_shapes=[
            pltpu.VMEM((nvars, depth, share * n), core.dtype),
            pltpu.VMEM((3, rows, share), core.dtype),
            pltpu.SemaphoreType.DMA((2, nvars, n)),
            pltpu.SemaphoreType.DMA((nvars, n)),
            pltpu.SemaphoreType.DMA((nvars,)),
            pltpu.SemaphoreType.DMA((3,)),
        ],
        compiler_params=pltpu.CompilerParams(
            collective_id=2, has_side_effects=True, vmem_limit_bytes=48 * 2**20
        ),
        name="rebuild_all",
    )(core, left_factor)


def highest(a, b, dims):
    return lax.dot_general(
        a,
        b,
        ((dims[:1], dims[1:]), ((), ())),
        precision=lax.Precision.HIGHEST,
        preferred_element_type=jnp.float32,
    )


def eliminate(block):
    size = block.shape[0]
    row = lax.broadcasted_iota(jnp.int32, block.shape, 0)
    scale = jnp.zeros_like(block)
    for j in range(size):
        column = jnp.broadcast_to(block[:, j:j + 1], block.shape)
        pivot = column[j:j + 1, :]
        scale = jnp.where(row == j, pivot, scale)
        if j < size - 1:
            step = column * (block[j:j + 1, :] / pivot)
            block = jnp.where(row > j, block - step, block)
    return block * lax.rsqrt(scale)


def orthonormal(block):
    size, nb = block.shape[1], 16
    small = highest(block, block, (0, 0))
    at = lax.broadcasted_iota(jnp.int32, (size, size), 0)
    to = lax.broadcasted_iota(jnp.int32, (size, size), 1)
    eye = (at == to).astype(jnp.float32)
    work = jnp.concatenate([small, eye], axis=1)
    inverse = []
    for k in range(0, size, nb):
        rows = work[k:k + nb, :]
        solved = eliminate(jnp.concatenate([rows[:, k:k + nb], eye[:nb, :nb]], axis=1))[:, nb:]
        panel = highest(solved, rows, (1, 0))
        inverse.append(panel[:, size:])
        if k + nb < size:
            work = work - highest(panel[:, :size], panel, (0, 0))
    return highest(block, jnp.concatenate(inverse, axis=0), (1, 1))


def iterate_kernel(gram, start, basis):
    basis[...] = orthonormal(start[...])

    @pl.loop(0, ITERS)
    def _(step):
        basis[...] = orthonormal(highest(gram[...], basis[...], (1, 0)))


def iterate(gram, start):
    return pl.pallas_call(
        iterate_kernel,
        out_shape=jax.ShapeDtypeStruct(start.shape, jnp.float32),
        in_specs=[VMEM, VMEM],
        out_specs=VMEM,
        compiler_params=pltpu.CompilerParams(vmem_limit_bytes=32 * 2**20),
        name="iterate",
    )(gram, start)


def on_device(sizes, field, rank, start_basis):
    nvars, rows, depth, width = field.shape
    n = sizes["fib"]
    flat = field.reshape(nvars, rows, depth * width)
    fibres, partial_gram = exchange(flat, n)
    gram = reduce_all(partial_gram, tuple((axis, sizes[axis]) for axis in ("var", "slab", "fib")))
    basis = iterate(gram, start_basis)
    columns = jnp.arange(basis.shape[1], dtype=jnp.int32)
    keep = (columns[None, :] < rank[:, None]).astype(basis.dtype)
    basis_bf = (basis[None, :, :] * keep[:, None, :]).astype(jnp.bfloat16)
    core = jnp.einsum("vir,vic->vrc", basis_bf, fibres, preferred_element_type=jnp.float32).astype(
        jnp.bfloat16
    )
    own_rows = lax.dynamic_slice_in_dim(basis_bf, lax.axis_index("fib") * rows, rows, 1)
    result = rebuild_all(core, own_rows, n)
    return result.reshape(nvars, rows, depth, width)


def solution(mesh):
    return jax.shard_map(
        functools.partial(on_device, dict(mesh.shape)),
        mesh=mesh,
        in_specs=(P(("grp", "var"), "fib", "slab", None), P(("grp", "var")), P()),
        out_specs=P(("grp", "var"), "fib", "slab", None),
        check_vma=False,
    )
```

```python
import functools

import jax
import jax.numpy as jnp
from jax import lax
from jax.experimental import pallas as pl
from jax.experimental.pallas import tpu as pltpu
from jax.sharding import PartitionSpec as P

ITERS = 4
MESH = pl.DeviceIdType.MESH
ANY = pl.BlockSpec(memory_space=pl.ANY)
VMEM = pl.BlockSpec(memory_space=pltpu.VMEM)
WINDOW = 3
CHUNK = 64
PARTS = (6, 8, 9, 10, 11, 12, 13, 14, 16)


def greet(axis, peers):
    barrier = pltpu.get_barrier_semaphore()
    for peer in peers:
        pl.semaphore_signal(barrier, inc=1, device_id={axis: peer}, device_id_type=MESH)
    pl.semaphore_wait(barrier, len(peers))


def exchange_kernel(n, flat, start_basis, fibres, gram, basis, held, send_sem, recv_sem, own_sem, load_sem):
    nvars, rows, _ = flat.shape
    share = fibres.shape[2]
    tile = min(share, 512)
    me = lax.axis_index("fib")
    greet("fib", [lax.rem(me + off, n) for off in range(1, n)])
    gram[...] = jnp.zeros_like(gram)

    def place(who, length):
        return pl.ds(pl.multiple_of(who * length, length), length)

    def remote(v, off):
        peer = lax.rem(me + off, n)
        return pltpu.make_async_remote_copy(
            src_ref=flat.at[v, :, place(peer, share)],
            dst_ref=fibres.at[v, place(me, rows), :],
            send_sem=send_sem.at[v, off],
            recv_sem=recv_sem.at[v, off],
            device_id={"fib": peer},
            device_id_type=MESH,
        )

    def arrival(v, off):
        source = lax.rem(me + n - off, n)
        return pltpu.make_async_remote_copy(
            src_ref=flat.at[v, :, place(me, share)],
            dst_ref=fibres.at[v, place(source, rows), :],
            send_sem=send_sem.at[v, off],
            recv_sem=recv_sem.at[v, off],
            device_id={"fib": lax.rem(me + off, n)},
            device_id_type=MESH,
        )

    def own(v):
        return pltpu.make_async_copy(
            flat.at[v, :, place(me, share)], fibres.at[v, place(me, rows), :], own_sem.at[v]
        )

    def start(v):
        own(v).start()
        pl.loop(1, n)(lambda off: remote(v, off).start())

    def finish(v):
        own(v).wait()

        @pl.loop(1, n)
        def _(off):
            remote(v, off).wait_send()
            arrival(v, off).wait_recv()

        load = pltpu.make_async_copy(fibres.at[v], held, load_sem)
        load.start()
        load.wait()

        @pl.loop(0, share // tile)
        def _(t):
            block = held[:, pl.ds(pl.multiple_of(t * tile, tile), tile)]
            gram[...] += lax.dot_general(
                block, block, (((1,), (1,)), ((), ())), preferred_element_type=jnp.float32
            )

    first = min(WINDOW, nvars)
    pl.loop(0, first)(start)
    basis[...] = orthonormal(start_basis[...])

    @pl.loop(first, nvars + WINDOW)
    def _(step):
        pl.when(step < nvars)(lambda: start(step))
        pl.when(step >= WINDOW)(lambda: finish(step - WINDOW))


def exchange(flat, start_basis, n):
    nvars, rows, columns = flat.shape
    whole, share = rows * n, columns // n
    return pl.pallas_call(
        functools.partial(exchange_kernel, n),
        out_shape=(
            jax.ShapeDtypeStruct((nvars, whole, share), flat.dtype),
            jax.ShapeDtypeStruct((whole, whole), jnp.float32),
            jax.ShapeDtypeStruct(start_basis.shape, jnp.float32),
        ),
        in_specs=[ANY, VMEM],
        out_specs=(ANY, VMEM, VMEM),
        scratch_shapes=[
            pltpu.VMEM((whole, share), flat.dtype),
            pltpu.SemaphoreType.DMA((nvars, n)),
            pltpu.SemaphoreType.DMA((nvars, n)),
            pltpu.SemaphoreType.DMA((nvars,)),
            pltpu.SemaphoreType.DMA,
        ],
        compiler_params=pltpu.CompilerParams(
            collective_id=0, has_side_effects=True, vmem_limit_bytes=32 * 2**20
        ),
        name="exchange",
    )(flat, start_basis)


def reduce_kernel(axes, part, total, held, *scratch):
    lands, sems = scratch[: len(axes)], scratch[len(axes):]
    barrier = pltpu.get_barrier_semaphore()
    count = 0
    for axis, n in axes:
        me = lax.axis_index(axis)
        for off in range(1, n):
            pl.semaphore_signal(
                barrier, inc=1, device_id={axis: lax.rem(me + off, n)}, device_id_type=MESH
            )
            count += 1
    pl.semaphore_wait(barrier, count)
    base, length = 0, total.shape[0]
    levels = []
    for level, (axis, n) in enumerate(axes):
        me = lax.axis_index(axis)
        size = length // n
        levels.append((axis, n, me, base, size))
        source = held if level else part
        copies = []
        for off in range(1, n):
            peer = lax.rem(me + off, n)
            copies.append(
                pltpu.make_async_remote_copy(
                    src_ref=source.at[pl.ds(pl.multiple_of(base + peer * size, size), size), :],
                    dst_ref=lands[level].at[off - 1],
                    send_sem=sems[0].at[level, off],
                    recv_sem=sems[1].at[level, off],
                    device_id={axis: peer},
                    device_id_type=MESH,
                )
            )
            copies[-1].start()
        base = base + me * size
        length = size
        for copy in copies:
            copy.wait()
        mine = pl.ds(pl.multiple_of(base, size), size)
        value = source[mine, :]
        for off in range(1, n):
            value += lands[level][off - 1]
        target = held if level < len(axes) - 1 else total
        target[mine, :] = value
    for level in reversed(range(len(axes))):
        axis, n, me, start, size = levels[level]
        mine = pl.ds(pl.multiple_of(start + me * size, size), size)
        sends = []
        for off in range(1, n):
            peer = lax.rem(me + off, n)
            sends.append(
                pltpu.make_async_remote_copy(
                    src_ref=total.at[mine, :],
                    dst_ref=total.at[mine, :],
                    send_sem=sems[2].at[level, off],
                    recv_sem=sems[3].at[level, off],
                    device_id={axis: peer},
                    device_id_type=MESH,
                )
            )
            sends[-1].start()
        for off in range(1, n):
            source = lax.rem(me + n - off, n)
            theirs = pl.ds(pl.multiple_of(start + source * size, size), size)
            sends[off - 1].wait_send()
            pltpu.make_async_remote_copy(
                src_ref=total.at[mine, :],
                dst_ref=total.at[theirs, :],
                send_sem=sems[2].at[level, off],
                recv_sem=sems[3].at[level, off],
                device_id={axis: lax.rem(me + off, n)},
                device_id_type=MESH,
            ).wait_recv()


def reduce_all(part, axes):
    rows, columns = part.shape
    total = 1
    for _, n in axes:
        total *= n
    if rows % (8 * total):
        return lax.psum(part, tuple(axis for axis, _ in axes))
    lands, size = [], rows
    for _, n in axes:
        size //= n
        lands.append(pltpu.VMEM((n - 1, size, columns), jnp.float32))
    sem = pltpu.SemaphoreType.DMA((len(axes), max(n for _, n in axes)))
    return pl.pallas_call(
        functools.partial(reduce_kernel, axes),
        out_shape=jax.ShapeDtypeStruct(part.shape, part.dtype),
        in_specs=[VMEM],
        out_specs=VMEM,
        scratch_shapes=[pltpu.VMEM(part.shape, jnp.float32)] + lands + [sem] * 4,
        compiler_params=pltpu.CompilerParams(
            collective_id=1, has_side_effects=True, vmem_limit_bytes=32 * 2**20
        ),
        name="reduce_all",
    )(part)


def rebuild_kernel(n, core, left_factor, out, full, stage, send_sem, recv_sem, own_sem, out_sem):
    packed, share = core.shape
    chunks = packed // CHUNK
    tile = min(share, 512)
    me = lax.axis_index("fib")
    barrier = pltpu.get_barrier_semaphore()
    has_left, has_right = me > 0, me < n - 1
    lo, hi = me - 1, me + 1

    for flag, peer in ((has_left, lo), (has_right, hi)):

        @pl.when(flag)
        def _():
            pl.semaphore_signal(barrier, inc=1, device_id={"fib": peer}, device_id_type=MESH)

    inner = has_left & has_right
    pl.when(inner)(lambda: pl.semaphore_wait(barrier, 2))
    pl.when(jnp.logical_not(inner))(lambda: pl.semaphore_wait(barrier, 1))

    def columns(who):
        return pl.ds(pl.multiple_of(who * share, share), share)

    def rows(c):
        return pl.ds(pl.multiple_of(c * CHUNK, CHUNK), CHUNK)

    def copy(c, who, side, peer):
        piece = full.at[rows(c), columns(who)]
        return pltpu.make_async_remote_copy(
            src_ref=piece,
            dst_ref=piece,
            send_sem=send_sem.at[side, c, who],
            recv_sem=recv_sem.at[c, who],
            device_id={"fib": peer},
            device_id_type=MESH,
        )

    def fetch(c):
        return pltpu.make_async_copy(
            core.at[rows(c), :], full.at[rows(c), columns(me)], own_sem.at[c]
        )

    def to_right(c, who):
        return copy(c, who, 1, hi)

    def to_left(c, who):
        return copy(c, who, 0, lo)

    def write(slot, who):
        return pltpu.make_async_copy(stage.at[slot], out.at[:, columns(who)], out_sem.at[slot])

    def rebuild(slot, who):
        @pl.loop(0, share // tile)
        def _(t):
            at = pl.ds(pl.multiple_of(t * tile, tile), tile)
            source = pl.ds(pl.multiple_of(who * share + t * tile, tile), tile)
            stage[slot, :, at] = jnp.dot(
                left_factor[...], full[:, source], preferred_element_type=jnp.float32
            ).astype(stage.dtype)

        write(slot, who).start()

    pl.loop(0, chunks)(lambda c: fetch(c).start())

    @pl.loop(0, chunks)
    def _(c):
        fetch(c).wait()
        pl.when(has_left)(lambda: to_left(c, me).start())
        pl.when(has_right)(lambda: to_right(c, me).start())

    rebuild(0, me)
    write(0, me).wait()

    @pl.loop(1, n)
    def _(hop):
        from_left, from_right = me - hop, me + hop
        left_ok, right_ok = from_left >= 0, from_right < n

        @pl.loop(0, chunks)
        def _(c):
            @pl.when(left_ok)
            def _():
                to_right(c, from_left).wait_recv()
                pl.when(has_right)(lambda: to_right(c, from_left).start())

            @pl.when(right_ok)
            def _():
                to_left(c, from_right).wait_recv()
                pl.when(has_left)(lambda: to_left(c, from_right).start())

        pl.when(left_ok)(lambda: rebuild(0, from_left))
        pl.when(right_ok)(lambda: rebuild(1, from_right))
        pl.when(left_ok)(lambda: write(0, from_left).wait())
        pl.when(right_ok)(lambda: write(1, from_right).wait())

    @pl.loop(0, n)
    def _(hop):
        from_left, from_right = me - hop, me + hop

        @pl.loop(0, chunks)
        def _(c):
            pl.when((from_left >= 0) & has_right)(lambda: to_right(c, from_left).wait_send())
            pl.when((from_right < n) & has_left)(lambda: to_left(c, from_right).wait_send())


def rebuild_all(core, left_factor, n, number):
    packed, share = core.shape
    rows = left_factor.shape[0]
    chunks = packed // CHUNK
    return pl.pallas_call(
        functools.partial(rebuild_kernel, n),
        out_shape=jax.ShapeDtypeStruct((rows, share * n), core.dtype),
        in_specs=[ANY, VMEM],
        out_specs=ANY,
        scratch_shapes=[
            pltpu.VMEM((packed, share * n), core.dtype),
            pltpu.VMEM((2, rows, share), core.dtype),
            pltpu.SemaphoreType.DMA((2, chunks, n)),
            pltpu.SemaphoreType.DMA((chunks, n)),
            pltpu.SemaphoreType.DMA((chunks,)),
            pltpu.SemaphoreType.DMA((2,)),
        ],
        compiler_params=pltpu.CompilerParams(
            collective_id=2 + number, has_side_effects=True, vmem_limit_bytes=48 * 2**20
        ),
        name=f"rebuild_all_{packed}",
    )(core, left_factor)


def project(number, packed, n, dims, basis, rank, fibres):
    nvars, rows, depth, width = dims
    end = jnp.cumsum(rank)
    begin = end - rank
    place = jnp.arange(packed, dtype=jnp.int32)
    owned = (place[None, :] >= begin[:, None]) & (place[None, :] < end[:, None])
    column = jnp.sum(jnp.where(owned, place[None, :] - begin[:, None], 0), axis=0)
    pick = (jnp.arange(basis.shape[1], dtype=jnp.int32)[:, None] == column[None, :]) & jnp.any(
        owned, axis=0
    )[None, :]
    chosen = jnp.dot(
        basis.astype(jnp.bfloat16), pick.astype(jnp.bfloat16), preferred_element_type=jnp.float32
    ).astype(jnp.bfloat16)
    mask = owned.astype(jnp.bfloat16)[:, None, :]
    core = jnp.einsum(
        "vim,vic->mc", chosen[None] * mask, fibres, preferred_element_type=jnp.float32
    ).astype(jnp.bfloat16)
    own = lax.dynamic_slice_in_dim(chosen, lax.axis_index("fib") * rows, rows, 0)
    left_factor = (own[None] * mask).reshape(nvars * rows, packed)
    return rebuild_all(core, left_factor, n, number).reshape(dims)


def highest(a, b, dims):
    return lax.dot_general(
        a,
        b,
        ((dims[:1], dims[1:]), ((), ())),
        precision=lax.Precision.HIGHEST,
        preferred_element_type=jnp.float32,
    )


def eliminate(block):
    size = block.shape[0]
    row = lax.broadcasted_iota(jnp.int32, block.shape, 0)
    scale = jnp.zeros_like(block)
    for j in range(size):
        column = jnp.broadcast_to(block[:, j:j + 1], block.shape)
        pivot = column[j:j + 1, :]
        scale = jnp.where(row == j, pivot, scale)
        if j < size - 1:
            step = column * (block[j:j + 1, :] / pivot)
            block = jnp.where(row > j, block - step, block)
    return block * lax.rsqrt(scale)


def orthonormal(block):
    size, nb = block.shape[1], 16
    small = highest(block, block, (0, 0))
    at = lax.broadcasted_iota(jnp.int32, (size, size), 0)
    to = lax.broadcasted_iota(jnp.int32, (size, size), 1)
    eye = (at == to).astype(jnp.float32)
    work = jnp.concatenate([small, eye], axis=1)
    inverse = []
    for k in range(0, size, nb):
        rows = work[k:k + nb, :]
        solved = eliminate(jnp.concatenate([rows[:, k:k + nb], eye[:nb, :nb]], axis=1))[:, nb:]
        panel = highest(solved, rows, (1, 0))
        inverse.append(panel[:, size:])
        if k + nb < size:
            work = work - highest(panel[:, :size], panel, (0, 0))
    return highest(block, jnp.concatenate(inverse, axis=0), (1, 1))


def iterate_kernel(gram, start, basis):
    basis[...] = start[...]

    @pl.loop(0, ITERS)
    def _(step):
        basis[...] = orthonormal(highest(gram[...], basis[...], (1, 0)))


def iterate(gram, start):
    return pl.pallas_call(
        iterate_kernel,
        out_shape=jax.ShapeDtypeStruct(start.shape, jnp.float32),
        in_specs=[VMEM, VMEM],
        out_specs=VMEM,
        compiler_params=pltpu.CompilerParams(vmem_limit_bytes=32 * 2**20),
        name="iterate",
    )(gram, start)


def on_device(sizes, field, rank, start_basis):
    nvars, rows, depth, width = field.shape
    n = sizes["fib"]
    needed = lax.pmax(jnp.sum(rank), tuple(sizes))
    flat = field.reshape(nvars, rows, depth * width)
    fibres, partial_gram, basis = exchange(flat, start_basis, n)
    gram = reduce_all(partial_gram, tuple((axis, sizes[axis]) for axis in ("var", "slab", "fib")))
    basis = iterate(gram, basis)
    most = nvars * basis.shape[1]
    widths = sorted({max(CHUNK, most * part // 16 // CHUNK * CHUNK) for part in PARTS})
    branches = [
        functools.partial(project, number, packed, n, field.shape)
        for number, packed in enumerate(widths)
    ]
    choice = sum((needed > packed).astype(jnp.int32) for packed in widths[:-1])
    return lax.switch(choice, branches, basis, rank, fibres)


def solution(mesh):
    return jax.shard_map(
        functools.partial(on_device, dict(mesh.shape)),
        mesh=mesh,
        in_specs=(P(("grp", "var"), "fib", "slab", None), P(("grp", "var")), P()),
        out_specs=P(("grp", "var"), "fib", "slab", None),
        check_vma=False,
    )
```

```python
import functools

import jax
import jax.numpy as jnp
from jax import lax
from jax.experimental import pallas as pl
from jax.experimental.pallas import tpu as pltpu
from jax.sharding import PartitionSpec as P

ITERS = 4
MESH = pl.DeviceIdType.MESH
ANY = pl.BlockSpec(memory_space=pl.ANY)
VMEM = pl.BlockSpec(memory_space=pltpu.VMEM)
WINDOW = 3


def greet(axis, peers):
    barrier = pltpu.get_barrier_semaphore()
    for peer in peers:
        pl.semaphore_signal(barrier, inc=1, device_id={axis: peer}, device_id_type=MESH)
    pl.semaphore_wait(barrier, len(peers))


def exchange_kernel(n, flat, start_basis, fibres, gram, basis, held, send_sem, recv_sem, own_sem, load_sem):
    nvars, rows, _ = flat.shape
    share = fibres.shape[2]
    tile = min(share, 512)
    me = lax.axis_index("fib")
    greet("fib", [lax.rem(me + off, n) for off in range(1, n)])
    gram[...] = jnp.zeros_like(gram)

    def place(who, length):
        return pl.ds(pl.multiple_of(who * length, length), length)

    def remote(v, off):
        peer = lax.rem(me + off, n)
        return pltpu.make_async_remote_copy(
            src_ref=flat.at[v, :, place(peer, share)],
            dst_ref=fibres.at[v, place(me, rows), :],
            send_sem=send_sem.at[v, off],
            recv_sem=recv_sem.at[v, off],
            device_id={"fib": peer},
            device_id_type=MESH,
        )

    def arrival(v, off):
        source = lax.rem(me + n - off, n)
        return pltpu.make_async_remote_copy(
            src_ref=flat.at[v, :, place(me, share)],
            dst_ref=fibres.at[v, place(source, rows), :],
            send_sem=send_sem.at[v, off],
            recv_sem=recv_sem.at[v, off],
            device_id={"fib": lax.rem(me + off, n)},
            device_id_type=MESH,
        )

    def own(v):
        return pltpu.make_async_copy(
            flat.at[v, :, place(me, share)], fibres.at[v, place(me, rows), :], own_sem.at[v]
        )

    def start(v):
        own(v).start()
        pl.loop(1, n)(lambda off: remote(v, off).start())

    def finish(v):
        own(v).wait()

        @pl.loop(1, n)
        def _(off):
            remote(v, off).wait_send()
            arrival(v, off).wait_recv()

        load = pltpu.make_async_copy(fibres.at[v], held, load_sem)
        load.start()
        load.wait()

        @pl.loop(0, share // tile)
        def _(t):
            block = held[:, pl.ds(pl.multiple_of(t * tile, tile), tile)]
            gram[...] += lax.dot_general(
                block, block, (((1,), (1,)), ((), ())), preferred_element_type=jnp.float32
            )

    first = min(WINDOW, nvars)
    pl.loop(0, first)(start)
    basis[...] = orthonormal(start_basis[...])

    @pl.loop(first, nvars + WINDOW)
    def _(step):
        pl.when(step < nvars)(lambda: start(step))
        pl.when(step >= WINDOW)(lambda: finish(step - WINDOW))


def exchange(flat, start_basis, n):
    nvars, rows, columns = flat.shape
    whole, share = rows * n, columns // n
    return pl.pallas_call(
        functools.partial(exchange_kernel, n),
        out_shape=(
            jax.ShapeDtypeStruct((nvars, whole, share), flat.dtype),
            jax.ShapeDtypeStruct((whole, whole), jnp.float32),
            jax.ShapeDtypeStruct(start_basis.shape, jnp.float32),
        ),
        in_specs=[ANY, VMEM],
        out_specs=(ANY, VMEM, VMEM),
        scratch_shapes=[
            pltpu.VMEM((whole, share), flat.dtype),
            pltpu.SemaphoreType.DMA((nvars, n)),
            pltpu.SemaphoreType.DMA((nvars, n)),
            pltpu.SemaphoreType.DMA((nvars,)),
            pltpu.SemaphoreType.DMA,
        ],
        compiler_params=pltpu.CompilerParams(
            collective_id=0, has_side_effects=True, vmem_limit_bytes=32 * 2**20
        ),
        name="exchange",
    )(flat, start_basis)


def reduce_kernel(axes, part, total, held, *scratch):
    lands, sems = scratch[: len(axes)], scratch[len(axes):]
    barrier = pltpu.get_barrier_semaphore()
    count = 0
    for axis, n in axes:
        me = lax.axis_index(axis)
        for off in range(1, n):
            pl.semaphore_signal(
                barrier, inc=1, device_id={axis: lax.rem(me + off, n)}, device_id_type=MESH
            )
            count += 1
    pl.semaphore_wait(barrier, count)
    base, length = 0, total.shape[0]
    levels = []
    for level, (axis, n) in enumerate(axes):
        me = lax.axis_index(axis)
        size = length // n
        levels.append((axis, n, me, base, size))
        source = held if level else part
        copies = []
        for off in range(1, n):
            peer = lax.rem(me + off, n)
            copies.append(
                pltpu.make_async_remote_copy(
                    src_ref=source.at[pl.ds(pl.multiple_of(base + peer * size, size), size), :],
                    dst_ref=lands[level].at[off - 1],
                    send_sem=sems[0].at[level, off],
                    recv_sem=sems[1].at[level, off],
                    device_id={axis: peer},
                    device_id_type=MESH,
                )
            )
            copies[-1].start()
        base = base + me * size
        length = size
        for copy in copies:
            copy.wait()
        mine = pl.ds(pl.multiple_of(base, size), size)
        value = source[mine, :]
        for off in range(1, n):
            value += lands[level][off - 1]
        target = held if level < len(axes) - 1 else total
        target[mine, :] = value
    for level in reversed(range(len(axes))):
        axis, n, me, start, size = levels[level]
        mine = pl.ds(pl.multiple_of(start + me * size, size), size)
        sends = []
        for off in range(1, n):
            peer = lax.rem(me + off, n)
            sends.append(
                pltpu.make_async_remote_copy(
                    src_ref=total.at[mine, :],
                    dst_ref=total.at[mine, :],
                    send_sem=sems[2].at[level, off],
                    recv_sem=sems[3].at[level, off],
                    device_id={axis: peer},
                    device_id_type=MESH,
                )
            )
            sends[-1].start()
        for off in range(1, n):
            source = lax.rem(me + n - off, n)
            theirs = pl.ds(pl.multiple_of(start + source * size, size), size)
            sends[off - 1].wait_send()
            pltpu.make_async_remote_copy(
                src_ref=total.at[mine, :],
                dst_ref=total.at[theirs, :],
                send_sem=sems[2].at[level, off],
                recv_sem=sems[3].at[level, off],
                device_id={axis: lax.rem(me + off, n)},
                device_id_type=MESH,
            ).wait_recv()


def reduce_all(part, axes):
    rows, columns = part.shape
    total = 1
    for _, n in axes:
        total *= n
    if rows % (8 * total):
        return lax.psum(part, tuple(axis for axis, _ in axes))
    lands, size = [], rows
    for _, n in axes:
        size //= n
        lands.append(pltpu.VMEM((n - 1, size, columns), jnp.float32))
    sem = pltpu.SemaphoreType.DMA((len(axes), max(n for _, n in axes)))
    return pl.pallas_call(
        functools.partial(reduce_kernel, axes),
        out_shape=jax.ShapeDtypeStruct(part.shape, part.dtype),
        in_specs=[VMEM],
        out_specs=VMEM,
        scratch_shapes=[pltpu.VMEM(part.shape, jnp.float32)] + lands + [sem] * 4,
        compiler_params=pltpu.CompilerParams(
            collective_id=1, has_side_effects=True, vmem_limit_bytes=32 * 2**20
        ),
        name="reduce_all",
    )(part)


def rebuild_kernel(n, core, left_factor, out, full, stage, send_sem, recv_sem, own_sem, out_sem):
    nvars, depth, share = core.shape
    rows = left_factor.shape[1]
    me = lax.axis_index("fib")
    barrier = pltpu.get_barrier_semaphore()
    has_left, has_right = me > 0, me < n - 1
    lo, hi = me - 1, me + 1

    for flag, peer in ((has_left, lo), (has_right, hi)):

        @pl.when(flag)
        def _():
            pl.semaphore_signal(barrier, inc=1, device_id={"fib": peer}, device_id_type=MESH)

    inner = has_left & has_right
    pl.when(inner)(lambda: pl.semaphore_wait(barrier, 2))
    pl.when(jnp.logical_not(inner))(lambda: pl.semaphore_wait(barrier, 1))

    def columns(who):
        return pl.ds(pl.multiple_of(who * share, share), share)

    def copy(v, who, side, peer):
        piece = full.at[v, :, columns(who)]
        return pltpu.make_async_remote_copy(
            src_ref=piece,
            dst_ref=piece,
            send_sem=send_sem.at[side, v, who],
            recv_sem=recv_sem.at[v, who],
            device_id={"fib": peer},
            device_id_type=MESH,
        )

    def fetch(v):
        return pltpu.make_async_copy(core.at[v], full.at[v, :, columns(me)], own_sem.at[v])

    def to_right(v, who):
        return copy(v, who, 1, hi)

    def to_left(v, who):
        return copy(v, who, 0, lo)

    def write(slot, v, who):
        return pltpu.make_async_copy(
            stage.at[slot], out.at[v, :, columns(who)], out_sem.at[slot]
        )

    def rebuild(slot, v, who, first):
        pl.when(jnp.logical_not(first))(lambda: write(slot, v, who).wait())
        tile = min(share, 512)

        @pl.loop(0, share // tile)
        def _(t):
            at = pl.ds(pl.multiple_of(t * tile, tile), tile)
            source = pl.ds(pl.multiple_of(who * share + t * tile, tile), tile)
            stage[slot, :, at] = jnp.dot(
                left_factor[v], full[v, :, source], preferred_element_type=jnp.float32
            ).astype(stage.dtype)

        write(slot, v, who).start()

    pl.loop(0, nvars)(lambda v: fetch(v).start())

    @pl.loop(0, nvars)
    def _(v):
        fetch(v).wait()
        pl.when(has_left)(lambda: to_left(v, me).start())
        pl.when(has_right)(lambda: to_right(v, me).start())

    pl.loop(0, nvars)(lambda v: rebuild(2, v, me, v == 0))
    write(2, 0, me).wait()

    for hop in range(1, n):
        from_left, from_right = me - hop, me + hop
        left_ok, right_ok = from_left >= 0, from_right < n

        @pl.loop(0, nvars)
        def _(v):
            @pl.when(left_ok)
            def _():
                to_right(v, from_left).wait_recv()
                pl.when(has_right)(lambda: to_right(v, from_left).start())

            @pl.when(right_ok)
            def _():
                to_left(v, from_right).wait_recv()
                pl.when(has_left)(lambda: to_left(v, from_right).start())

            pl.when(left_ok)(lambda: rebuild(0, v, from_left, v == 0))
            pl.when(right_ok)(lambda: rebuild(1, v, from_right, v == 0))

        pl.when(left_ok)(lambda: write(0, 0, from_left).wait())
        pl.when(right_ok)(lambda: write(1, 0, from_right).wait())

    for hop in range(n):
        from_left, from_right = me - hop, me + hop

        @pl.loop(0, nvars)
        def _(v):
            pl.when((from_left >= 0) & has_right)(lambda: to_right(v, from_left).wait_send())
            pl.when((from_right < n) & has_left)(lambda: to_left(v, from_right).wait_send())


def rebuild_all(core, left_factor, n):
    nvars, depth, share = core.shape
    rows = left_factor.shape[1]
    return pl.pallas_call(
        functools.partial(rebuild_kernel, n),
        out_shape=jax.ShapeDtypeStruct((nvars, rows, share * n), core.dtype),
        in_specs=[ANY, VMEM],
        out_specs=ANY,
        scratch_shapes=[
            pltpu.VMEM((nvars, depth, share * n), core.dtype),
            pltpu.VMEM((3, rows, share), core.dtype),
            pltpu.SemaphoreType.DMA((2, nvars, n)),
            pltpu.SemaphoreType.DMA((nvars, n)),
            pltpu.SemaphoreType.DMA((nvars,)),
            pltpu.SemaphoreType.DMA((3,)),
        ],
        compiler_params=pltpu.CompilerParams(
            collective_id=2, has_side_effects=True, vmem_limit_bytes=48 * 2**20
        ),
        name="rebuild_all",
    )(core, left_factor)


def highest(a, b, dims):
    return lax.dot_general(
        a,
        b,
        ((dims[:1], dims[1:]), ((), ())),
        precision=lax.Precision.HIGHEST,
        preferred_element_type=jnp.float32,
    )


def eliminate(block):
    size = block.shape[0]
    row = lax.broadcasted_iota(jnp.int32, block.shape, 0)
    scale = jnp.zeros_like(block)
    for j in range(size):
        column = jnp.broadcast_to(block[:, j:j + 1], block.shape)
        pivot = column[j:j + 1, :]
        scale = jnp.where(row == j, pivot, scale)
        if j < size - 1:
            step = column * (block[j:j + 1, :] / pivot)
            block = jnp.where(row > j, block - step, block)
    return block * lax.rsqrt(scale)


def orthonormal(block):
    size, nb = block.shape[1], 16
    small = highest(block, block, (0, 0))
    at = lax.broadcasted_iota(jnp.int32, (size, size), 0)
    to = lax.broadcasted_iota(jnp.int32, (size, size), 1)
    eye = (at == to).astype(jnp.float32)
    work = jnp.concatenate([small, eye], axis=1)
    inverse = []
    for k in range(0, size, nb):
        rows = work[k:k + nb, :]
        solved = eliminate(jnp.concatenate([rows[:, k:k + nb], eye[:nb, :nb]], axis=1))[:, nb:]
        panel = highest(solved, rows, (1, 0))
        inverse.append(panel[:, size:])
        if k + nb < size:
            work = work - highest(panel[:, :size], panel, (0, 0))
    return highest(block, jnp.concatenate(inverse, axis=0), (1, 1))


def iterate_kernel(gram, start, basis):
    basis[...] = start[...]

    @pl.loop(0, ITERS)
    def _(step):
        basis[...] = orthonormal(highest(gram[...], basis[...], (1, 0)))


def iterate(gram, start):
    return pl.pallas_call(
        iterate_kernel,
        out_shape=jax.ShapeDtypeStruct(start.shape, jnp.float32),
        in_specs=[VMEM, VMEM],
        out_specs=VMEM,
        compiler_params=pltpu.CompilerParams(vmem_limit_bytes=32 * 2**20),
        name="iterate",
    )(gram, start)


def on_device(sizes, field, rank, start_basis):
    nvars, rows, depth, width = field.shape
    n = sizes["fib"]
    flat = field.reshape(nvars, rows, depth * width)
    fibres, partial_gram, basis = exchange(flat, start_basis, n)
    gram = reduce_all(partial_gram, tuple((axis, sizes[axis]) for axis in ("var", "slab", "fib")))
    basis = iterate(gram, basis)
    columns = jnp.arange(basis.shape[1], dtype=jnp.int32)
    keep = (columns[None, :] < rank[:, None]).astype(basis.dtype)
    basis_bf = (basis[None, :, :] * keep[:, None, :]).astype(jnp.bfloat16)
    core = jnp.einsum("vir,vic->vrc", basis_bf, fibres, preferred_element_type=jnp.float32).astype(
        jnp.bfloat16
    )
    own_rows = lax.dynamic_slice_in_dim(basis_bf, lax.axis_index("fib") * rows, rows, 1)
    result = rebuild_all(core, own_rows, n)
    return result.reshape(nvars, rows, depth, width)


def solution(mesh):
    return jax.shard_map(
        functools.partial(on_device, dict(mesh.shape)),
        mesh=mesh,
        in_specs=(P(("grp", "var"), "fib", "slab", None), P(("grp", "var")), P()),
        out_specs=P(("grp", "var"), "fib", "slab", None),
        check_vma=False,
    )
```
